32 devices in a mesh: rows: 8 (over z, core), cols: 4 (over y, x).
Axes of the slice: x: 2, y: 2, z: 4, core: 2. Of those that a mesh axis runs over, the one named last changes fastest.
Arguments:
- markov: bfloat16 [2048, 4096], P('rows'), may hold values from -0.015625 to 0.015625
- panel: bfloat16 [131072, 256], P('rows'), may hold values from -6 to 6
Outputs:
- product: float32 [4, 4096, 256], P('cols', 'rows')
The draws below stay inside these ranges and needn't reach their ends.
All inputs are finite; a program needn't handle non-finite values.
Results may differ from the reference program's by a relative error of at most 0.0003.
Values may be sent and summed in bfloat16 or wider, within the bound.
A program may use at most 128 MiB of HBM per device.

```python
import jax
import jax.numpy as jnp
from jax import lax

P_SIZE = 64
M = 64
K = 256
NBR = 2048
NBC = 256
BCD = 64
N_COLS = 4


def shard_levels(key, shape, pieces, smallest, largest):
    factor_of, own = 1.0, jax.random.fold_in(key, 6)
    for dim, blocks in pieces:
        draws = jnp.exp(jax.random.uniform(jax.random.fold_in(own, dim), (blocks,), jnp.float32, smallest / len(pieces), largest / len(pieces)))
        factor_of = factor_of * jnp.repeat(draws, shape[dim] // blocks).reshape([-1 if axis == dim else 1 for axis in range(len(shape))])
    return factor_of


def centred(own_key, dims, spread, reach, cuts=(), kind=jnp.bfloat16):
    array = spread * jax.random.normal(own_key, dims, jnp.float32)
    if cuts:
        array = array * shard_levels(own_key, dims, cuts, -0.22, 0.18)
    return jnp.clip(array, -reach, reach).astype(kind)


def setup_inputs(seed: int = 0) -> dict:
    streams_of = jax.random.split(jax.random.key(seed), 3)
    markov = centred(streams_of[0], (NBR, P_SIZE * M), (NBR * P_SIZE) ** -0.5, 0.015625, ((0, 8),))
    panel = centred(streams_of[1], (NBR * P_SIZE, K), 1.0, 6.0, ((0, 8),))
    return {"markov": markov, "panel": panel}


def reference(markov, panel):
    doubled = jnp.concatenate([markov, markov[:NBC]], 0).astype(jnp.float32)
    queries = panel.astype(jnp.float32)

    def column(index):
        tile = lax.dynamic_slice_in_dim(doubled, index, NBR, 0).reshape(NBR * P_SIZE, M)
        return jnp.dot(tile.T, queries, precision=lax.Precision.HIGHEST, preferred_element_type=jnp.float32)

    blocks = lax.map(column, jnp.arange(NBC, dtype=jnp.int32))
    return blocks.reshape(N_COLS, BCD * M, K)
```

```python
import functools

import jax
import jax.numpy as jnp
from jax import lax
from jax.experimental import pallas as pl
from jax.experimental.pallas import tpu as pltpu
from jax.sharding import PartitionSpec as P

MESH = pl.DeviceIdType.MESH


def kernel(
    n, inputs, blocks_owned, pieces, depth,
    ll_ref, q_hbm, out_ref,
    q_ref, give, got, acc, from_left, from_right,
    q_sem, give_sem, got_sem, line_sem, left_sem, right_sem,
):
    line = n // 2
    steps = line * pieces
    chunks = q_hbm.shape[0] // depth
    per_piece = blocks_owned // pieces
    rows_piece = per_piece * inputs
    row = lax.axis_index("rows")
    here, core = row // 2, lax.rem(row, 2)
    sibling = row + 1 - 2 * core
    has_left, has_right = here > 0, here < line - 1

    def q_copy(c):
        where = pl.ds(pl.multiple_of(c * depth, depth), depth)
        return pltpu.make_async_copy(q_hbm.at[where], q_ref.at[where], q_sem.at[c])

    @pl.loop(0, chunks)
    def _(c):
        q_copy(c).start()

    barrier = pltpu.get_barrier_semaphore()

    def greet(target):
        pl.semaphore_signal(barrier, inc=1, device_id={"rows": target}, device_id_type=MESH)

    greet(sibling)
    pl.when(has_left)(lambda: greet(row - 2))
    pl.when(has_right)(lambda: greet(row + 2))
    pl.semaphore_wait(barrier, 1 + jnp.where(has_left, 1, 0) + jnp.where(has_right, 1, 0))

    def target_of(step):
        k = step // pieces
        low = here < line // 2
        h = jnp.where(low, here, line - 1 - here)
        d = jnp.where(k < line - 1 - h, line - 1 - k, jnp.where(k < line - 1, k - (line - 1 - h), h))
        return jnp.where(low, d, line - 1 - d)

    def tile(step, core_of, dst, first):
        d, piece = target_of(step), lax.rem(step, pieces)
        start = ((2 * d + core_of) * blocks_owned + piece * per_piece) * inputs
        dst[...] = jnp.zeros_like(dst)

        @pl.loop(0, chunks)
        def _(c):
            if first is not None:
                pl.when(first)(lambda: q_copy(c).wait())
            weights = q_ref[pl.ds(pl.multiple_of(c * depth, depth), depth), :]
            parts = [
                ll_ref[:, pl.ds(pl.multiple_of(start + c * depth + 2 * inputs * p, 128), depth)]
                for p in range(per_piece // 2)
            ]
            lhs = jnp.concatenate(parts, 0) if len(parts) > 1 else parts[0]
            dst[...] += jnp.dot(lhs, weights, preferred_element_type=jnp.float32)

    def give_copy(step):
        return pltpu.make_async_remote_copy(
            give.at[step], got.at[step], give_sem.at[step], got_sem.at[step],
            device_id={"rows": sibling}, device_id_type=MESH,
        )

    def right_copy(step, slot):
        return pltpu.make_async_remote_copy(
            acc.at[step], from_left.at[slot], line_sem.at[step], left_sem.at[slot],
            device_id={"rows": row + 2}, device_id_type=MESH,
        )

    def left_copy(step, slot):
        return pltpu.make_async_remote_copy(
            acc.at[step], from_right.at[slot], line_sem.at[step], right_sem.at[slot],
            device_id={"rows": row - 2}, device_id_type=MESH,
        )

    def combine(step):
        d, piece = target_of(step), lax.rem(step, pieces)
        slot = d * pieces + piece
        give_copy(step).wait_recv()
        acc[step] += got[step]

        @pl.when(jnp.logical_and(d >= here, has_left))
        def _():
            right_copy(step, slot).wait_recv()
            acc[step] += from_left[slot]

        @pl.when(jnp.logical_and(d <= here, has_right))
        def _():
            left_copy(step, slot).wait_recv()
            acc[step] += from_right[slot]

        pl.when(d > here)(lambda: right_copy(step, slot).start())
        pl.when(d < here)(lambda: left_copy(step, slot).start())

        @pl.when(d == here)
        def _():
            out_ref[pl.ds(pl.multiple_of(piece * rows_piece, rows_piece), rows_piece), :] = acc[step]

    @pl.loop(0, steps)
    def _(step):
        tile(step, 1 - core, give.at[step], step == 0)
        give_copy(step).start()
        tile(step, core, acc.at[step], None)
        pl.when(step > 0)(lambda: combine(step - 1))

    combine(steps - 1)

    @pl.loop(0, steps)
    def _(step):
        d, piece = target_of(step), lax.rem(step, pieces)
        slot = d * pieces + piece
        give_copy(step).wait_send()
        pl.when(d > here)(lambda: right_copy(step, slot).wait_send())
        pl.when(d < here)(lambda: left_copy(step, slot).wait_send())


def per_device(markov, panel):
    rows_here = markov.shape[0]
    n = lax.axis_size("rows")
    width_cols = rows_here // lax.axis_size("cols")
    sensors = panel.shape[0] // rows_here
    inputs = markov.shape[1] // sensors
    k = panel.shape[1]
    base = lax.axis_index("cols") * width_cols
    after = lax.ppermute(markov, "rows", [(i, (i - 1) % n) for i in range(n)])
    joined = jnp.concatenate([markov, after], 0)
    needed = lax.dynamic_slice_in_dim(joined, base, rows_here + width_cols, 0)
    count = rows_here + width_cols
    flat = needed.reshape(count, sensors, inputs).transpose(2, 0, 1).reshape(inputs, count * sensors)
    moved = jnp.concatenate([flat[:, sensors:], flat[:, :sensors]], 1)
    ll = jnp.concatenate([flat, moved], 0)

    blocks_owned = width_cols // n
    pieces = 2 if blocks_owned % 4 == 0 else 1
    depth = 2048
    steps = (n // 2) * pieces
    tile = (steps, blocks_owned * inputs // pieces, k)
    dma = pltpu.SemaphoreType.DMA
    mine = pl.pallas_call(
        functools.partial(kernel, n, inputs, blocks_owned, pieces, depth),
        out_shape=jax.ShapeDtypeStruct((blocks_owned * inputs, k), jnp.float32),
        in_specs=[pl.BlockSpec(memory_space=pltpu.VMEM), pl.BlockSpec(memory_space=pl.ANY)],
        out_specs=pl.BlockSpec(memory_space=pltpu.VMEM),
        scratch_shapes=[pltpu.VMEM(panel.shape, jnp.bfloat16)]
        + [pltpu.VMEM(tile, jnp.float32)] * 5
        + [dma((panel.shape[0] // depth,))]
        + [dma((steps,))] * 5,
        compiler_params=pltpu.CompilerParams(
            collective_id=0, has_side_effects=True, vmem_limit_bytes=56 * 2**20
        ),
        cost_estimate=pl.CostEstimate(
            flops=2 * width_cols * inputs * panel.shape[0] * k, bytes_accessed=16 * 2**20, transcendentals=0
        ),
    )(ll, panel)
    return mine[None]


def solution(mesh):
    placed = (P("rows", None), P("rows", None))
    return jax.shard_map(
        per_device, mesh=mesh, in_specs=placed, out_specs=P("cols", "rows", None), check_vma=False
    )
```

```python
import functools

import jax
import jax.numpy as jnp
from jax import lax
from jax.experimental import pallas as pl
from jax.experimental.pallas import tpu as pltpu
from jax.sharding import PartitionSpec as P

MESH = pl.DeviceIdType.MESH


def kernel(
    n, cols, inputs, blocks_owned, pieces,
    markov_hbm, q_hbm, out_ref,
    raw, spread, expand, ll_ref,
    q_ref, give, got, acc, from_left, from_right,
    near_sem, away_sem, next_sem, q_sem, give_sem, got_sem, line_sem, left_sem, right_sem,
):
    line = n // 2
    steps = line * pieces
    per_piece = blocks_owned // pieces
    rows_piece = per_piece * inputs
    width = markov_hbm.shape[0] // cols
    sensors = q_hbm.shape[0] // markov_hbm.shape[0]
    first_depth = width * sensors
    row, col = lax.axis_index("rows"), lax.axis_index("cols")
    here, core = row // 2, lax.rem(row, 2)
    sibling = row + 1 - 2 * core
    before, behind = lax.rem(row + n - 1, n), lax.rem(row + 1, n)
    has_left, has_right = here > 0, here < line - 1

    def q_copy(part):
        where = pl.ds(0, first_depth) if part == 0 else pl.ds(first_depth, q_hbm.shape[0] - first_depth)
        return pltpu.make_async_copy(q_hbm.at[where], q_ref.at[where], q_sem.at[part])

    def near_copy(g):
        src = pl.ds(pl.multiple_of((col + g) * width, width), width)
        dst = pl.ds(pl.multiple_of(g * width, width), width)
        return pltpu.make_async_copy(markov_hbm.at[src], raw.at[dst], near_sem.at[g])

    def next_copy(e):
        src = pl.ds(pl.multiple_of(e * width, width), width)
        dst = pl.ds(pl.multiple_of((e + cols - col) * width, width), width)
        return pltpu.make_async_remote_copy(
            markov_hbm.at[src], raw.at[dst], away_sem.at[e], next_sem.at[e],
            device_id={"rows": before}, device_id_type=MESH,
        )

    @pl.loop(0, cols - col)
    def _(g):
        near_copy(g).start()

    q_copy(0).start()
    q_copy(1).start()
    barrier = pltpu.get_barrier_semaphore()

    def greet(target):
        pl.semaphore_signal(barrier, inc=1, device_id={"rows": target}, device_id_type=MESH)

    greet(before)
    greet(behind)
    pl.when(has_left)(lambda: greet(row - 2))
    pl.when(has_right)(lambda: greet(row + 2))
    pl.semaphore_wait(barrier, 2 + jnp.where(has_left, 1, 0) + jnp.where(has_right, 1, 0))

    @pl.loop(0, col + 1)
    def _(e):
        next_copy(e).start()

    lane = 128
    half = expand.shape[0] // 2
    x = lax.broadcasted_iota(jnp.int32, expand.shape, 0)
    y = lax.broadcasted_iota(jnp.int32, expand.shape, 1)
    expand[...] = jnp.where(y == jnp.where(x < half, 2 * x, 2 * (x - half) + 1), 1.0, 0.0).astype(jnp.bfloat16)
    ll_ref[:, 0:lane] = jnp.zeros((2 * inputs, lane), jnp.bfloat16)
    group = 16
    pairs = sensors // 2

    def lay_out(g):
        pl.when(col + g < cols)(lambda: near_copy(g).wait())
        pl.when(col + g >= cols)(lambda: next_copy(col + g - cols).wait_recv())

        @pl.loop(0, width // group)
        def _(i):
            at = pl.multiple_of(g * width + i * group, group)
            for c in range(pairs):
                spread[pl.ds(c, group, stride=pairs), :] = raw[
                    pl.ds(at, group), c * lane : (c + 1) * lane
                ].astype(jnp.float32)
            turned = spread[...].astype(jnp.bfloat16).T
            lhs = jnp.concatenate(
                [
                    jnp.concatenate([turned[:inputs, k * half : (k + 1) * half], turned[inputs:, k * half : (k + 1) * half]], 1)
                    for k in range(2)
                ],
                0,
            )
            done = jnp.dot(lhs, expand[...], preferred_element_type=jnp.float32).astype(jnp.bfloat16)
            for k in range(2):
                to = pl.multiple_of(lane + at * sensors + k * 2 * half, lane)
                ll_ref[0:inputs, pl.ds(to, 2 * half)] = done[k * inputs : (k + 1) * inputs]

        span = 512

        @pl.loop(0, width * sensors // span)
        def _(i):
            at = pl.multiple_of(g * width * sensors + i * span, lane)
            wide = ll_ref[0:inputs, pl.ds(at, span + lane)]
            ll_ref[inputs : 2 * inputs, pl.ds(at, span)] = wide[:, sensors : sensors + span]

    def target_of(step):
        k = step // pieces
        low = here < line // 2
        h = jnp.where(low, here, line - 1 - here)
        d = jnp.where(k < line - 1 - h, line - 1 - k, jnp.where(k < line - 1, k - (line - 1 - h), h))
        return jnp.where(low, d, line - 1 - d)

    def part_of(step, core_of, begin, depth):
        d, piece = target_of(step), lax.rem(step, pieces)
        start = ((2 * d + core_of) * blocks_owned + piece * per_piece) * inputs + lane + begin
        parts = [
            ll_ref[:, pl.ds(pl.multiple_of(start + 2 * inputs * p, lane), depth)]
            for p in range(per_piece // 2)
        ]
        lhs = jnp.concatenate(parts, 0) if len(parts) > 1 else parts[0]
        return jnp.dot(lhs, q_ref[begin : begin + depth, :], preferred_element_type=jnp.float32)

    def give_copy(step):
        return pltpu.make_async_remote_copy(
            give.at[step], got.at[step], give_sem.at[step], got_sem.at[step],
            device_id={"rows": sibling}, device_id_type=MESH,
        )

    def right_copy(step, slot):
        return pltpu.make_async_remote_copy(
            acc.at[step], from_left.at[slot], line_sem.at[step], left_sem.at[slot],
            device_id={"rows": row + 2}, device_id_type=MESH,
        )

    def left_copy(step, slot):
        return pltpu.make_async_remote_copy(
            acc.at[step], from_right.at[slot], line_sem.at[step], right_sem.at[slot],
            device_id={"rows": row - 2}, device_id_type=MESH,
        )

    def combine(step):
        d, piece = target_of(step), lax.rem(step, pieces)
        slot = d * pieces + piece
        give_copy(step).wait_recv()
        acc[step] += got[step]

        @pl.when(jnp.logical_and(d >= here, has_left))
        def _():
            right_copy(step, slot).wait_recv()
            acc[step] += from_left[slot]

        @pl.when(jnp.logical_and(d <= here, has_right))
        def _():
            left_copy(step, slot).wait_recv()
            acc[step] += from_right[slot]

        pl.when(d > here)(lambda: right_copy(step, slot).start())
        pl.when(d < here)(lambda: left_copy(step, slot).start())

        @pl.when(d == here)
        def _():
            out_ref[pl.ds(pl.multiple_of(piece * rows_piece, rows_piece), rows_piece), :] = acc[step]

    pl.loop(0, 2)(lay_out)
    q_copy(0).wait()

    @pl.loop(0, steps)
    def _(step):
        give[step] = part_of(step, 1 - core, 0, first_depth)
        acc[step] = part_of(step, core, 0, first_depth)

    pl.loop(2, cols + 1)(lay_out)
    q_copy(1).wait()
    rest = q_hbm.shape[0] - first_depth

    @pl.loop(0, steps)
    def _(step):
        give[step] += part_of(step, 1 - core, first_depth, rest)
        give_copy(step).start()
        acc[step] += part_of(step, core, first_depth, rest)
        pl.when(step > 0)(lambda: combine(step - 1))

    combine(steps - 1)

    @pl.loop(0, steps)
    def _(step):
        d, piece = target_of(step), lax.rem(step, pieces)
        slot = d * pieces + piece
        give_copy(step).wait_send()
        pl.when(d > here)(lambda: right_copy(step, slot).wait_send())
        pl.when(d < here)(lambda: left_copy(step, slot).wait_send())

    @pl.loop(0, col + 1)
    def _(e):
        next_copy(e).wait_send()


def per_device(markov, panel):
    rows_here = markov.shape[0]
    n = lax.axis_size("rows")
    width_cols = rows_here // lax.axis_size("cols")
    sensors = panel.shape[0] // rows_here
    inputs = markov.shape[1] // sensors
    k = panel.shape[1]
    cols = lax.axis_size("cols")
    blocks_owned = width_cols // n
    pieces = 2 if blocks_owned % 4 == 0 else 1
    steps = (n // 2) * pieces
    tile = (steps, blocks_owned * inputs // pieces, k)
    dma = pltpu.SemaphoreType.DMA
    mine = pl.pallas_call(
        functools.partial(kernel, n, cols, inputs, blocks_owned, pieces),
        out_shape=jax.ShapeDtypeStruct((blocks_owned * inputs, k), jnp.float32),
        in_specs=[pl.BlockSpec(memory_space=pl.ANY)] * 2,
        out_specs=pl.BlockSpec(memory_space=pltpu.VMEM),
        scratch_shapes=[
            pltpu.VMEM((rows_here + width_cols, sensors * inputs), jnp.bfloat16),
            pltpu.VMEM((16 * sensors // 2, 128), jnp.float32),
            pltpu.VMEM((8 * sensors, 8 * sensors), jnp.bfloat16),
            pltpu.VMEM((2 * inputs, 128 + (rows_here + width_cols) * sensors), jnp.bfloat16),
            pltpu.VMEM(panel.shape, jnp.bfloat16),
        ]
        + [pltpu.VMEM(tile, jnp.float32)] * 5
        + [dma((cols,))] * 3
        + [dma((2,))]
        + [dma((steps,))] * 5,
        compiler_params=pltpu.CompilerParams(
            collective_id=0, has_side_effects=True, vmem_limit_bytes=56 * 2**20
        ),
        cost_estimate=pl.CostEstimate(
            flops=2 * width_cols * inputs * panel.shape[0] * k, bytes_accessed=16 * 2**20, transcendentals=0
        ),
    )(markov, panel)
    return mine[None]


def solution(mesh):
    placed = (P("rows", None), P("rows", None))
    return jax.shard_map(
        per_device, mesh=mesh, in_specs=placed, out_specs=P("cols", "rows", None), check_vma=False
    )
```

```python
import functools

import jax
import jax.numpy as jnp
from jax import lax
from jax.experimental import pallas as pl
from jax.experimental.pallas import tpu as pltpu
from jax.sharding import PartitionSpec as P

MESH = pl.DeviceIdType.MESH


def kernel(
    n, cols, inputs, blocks_owned, pieces,
    markov_hbm, q_hbm, out_ref,
    raw, spread, expand, ll_ref,
    q_ref, give, got, acc, from_left, from_right,
    near_sem, away_sem, next_sem, q_sem, give_sem, got_sem, line_sem, left_sem, right_sem,
):
    line = n // 2
    steps = line * pieces
    per_piece = blocks_owned // pieces
    rows_piece = per_piece * inputs
    width = markov_hbm.shape[0] // cols
    sensors = q_hbm.shape[0] // markov_hbm.shape[0]
    first_depth = width * sensors
    row, col = lax.axis_index("rows"), lax.axis_index("cols")
    here, core = row // 2, lax.rem(row, 2)
    sibling = row + 1 - 2 * core
    before, behind = lax.rem(row + n - 1, n), lax.rem(row + 1, n)
    has_left, has_right = here > 0, here < line - 1

    def q_copy(part):
        where = pl.ds(0, first_depth) if part == 0 else pl.ds(first_depth, q_hbm.shape[0] - first_depth)
        return pltpu.make_async_copy(q_hbm.at[where], q_ref.at[where], q_sem.at[part])

    def near_copy(g):
        src = pl.ds(pl.multiple_of((col + g) * width, width), width)
        dst = pl.ds(pl.multiple_of(g * width, width), width)
        return pltpu.make_async_copy(markov_hbm.at[src], raw.at[dst], near_sem.at[g])

    def next_copy(e):
        src = pl.ds(pl.multiple_of(e * width, width), width)
        dst = pl.ds(pl.multiple_of((e + cols - col) * width, width), width)
        return pltpu.make_async_remote_copy(
            markov_hbm.at[src], raw.at[dst], away_sem.at[e], next_sem.at[e],
            device_id={"rows": before}, device_id_type=MESH,
        )

    @pl.loop(0, cols - col)
    def _(g):
        near_copy(g).start()

    q_copy(0).start()
    q_copy(1).start()
    barrier = pltpu.get_barrier_semaphore()

    def greet(target):
        pl.semaphore_signal(barrier, inc=1, device_id={"rows": target}, device_id_type=MESH)

    greet(before)
    greet(behind)
    pl.when(has_left)(lambda: greet(row - 2))
    pl.when(has_right)(lambda: greet(row + 2))
    pl.semaphore_wait(barrier, 2 + jnp.where(has_left, 1, 0) + jnp.where(has_right, 1, 0))

    @pl.loop(0, col + 1)
    def _(e):
        next_copy(e).start()

    lane = 128
    half = expand.shape[0] // 2
    x = lax.broadcasted_iota(jnp.int32, expand.shape, 0)
    y = lax.broadcasted_iota(jnp.int32, expand.shape, 1)
    expand[...] = jnp.where(y == jnp.where(x < half, 2 * x, 2 * (x - half) + 1), 1.0, 0.0).astype(jnp.bfloat16)
    ll_ref[:, 0:lane] = jnp.zeros((2 * inputs, lane), jnp.bfloat16)
    group = 32
    pairs = sensors // 2

    def lay_out(g):
        pl.when(col + g < cols)(lambda: near_copy(g).wait())
        pl.when(col + g >= cols)(lambda: next_copy(col + g - cols).wait_recv())

        @pl.loop(0, width // group)
        def _(i):
            at = pl.multiple_of(g * width + i * group, group)
            for c in range(pairs):
                spread[pl.ds(c, group, stride=pairs), :] = raw[
                    pl.ds(at, group), c * lane : (c + 1) * lane
                ].astype(jnp.float32)
            turned = spread[...].astype(jnp.bfloat16).T
            lhs = jnp.concatenate(
                [
                    jnp.concatenate([turned[:inputs, k * half : (k + 1) * half], turned[inputs:, k * half : (k + 1) * half]], 1)
                    for k in range(2 * group // 16)
                ],
                0,
            )
            done = jnp.dot(lhs, expand[...], preferred_element_type=jnp.float32).astype(jnp.bfloat16)
            for k in range(2 * group // 16):
                to = pl.multiple_of(lane + at * sensors + k * 2 * half, lane)
                ll_ref[0:inputs, pl.ds(to, 2 * half)] = done[k * inputs : (k + 1) * inputs]

        span = 512

        @pl.loop(0, width * sensors // span)
        def _(i):
            at = pl.multiple_of(g * width * sensors + i * span, lane)
            wide = ll_ref[0:inputs, pl.ds(at, span + lane)]
            ll_ref[inputs : 2 * inputs, pl.ds(at, span)] = wide[:, sensors : sensors + span]

    def target_of(step):
        k = step // pieces
        low = here < line // 2
        h = jnp.where(low, here, line - 1 - here)
        d = jnp.where(k < line - 1 - h, line - 1 - k, jnp.where(k < line - 1, k - (line - 1 - h), h))
        return jnp.where(low, d, line - 1 - d)

    def part_of(step, core_of, begin, depth):
        d, piece = target_of(step), lax.rem(step, pieces)
        start = ((2 * d + core_of) * blocks_owned + piece * per_piece) * inputs + lane + begin
        parts = [
            ll_ref[:, pl.ds(pl.multiple_of(start + 2 * inputs * p, lane), depth)]
            for p in range(per_piece // 2)
        ]
        lhs = jnp.concatenate(parts, 0) if len(parts) > 1 else parts[0]
        return jnp.dot(lhs, q_ref[begin : begin + depth, :], preferred_element_type=jnp.float32)

    def give_copy(step):
        return pltpu.make_async_remote_copy(
            give.at[step], got.at[step], give_sem.at[step], got_sem.at[step],
            device_id={"rows": sibling}, device_id_type=MESH,
        )

    def right_copy(step, slot):
        return pltpu.make_async_remote_copy(
            acc.at[step], from_left.at[slot], line_sem.at[step], left_sem.at[slot],
            device_id={"rows": row + 2}, device_id_type=MESH,
        )

    def left_copy(step, slot):
        return pltpu.make_async_remote_copy(
            acc.at[step], from_right.at[slot], line_sem.at[step], right_sem.at[slot],
            device_id={"rows": row - 2}, device_id_type=MESH,
        )

    def awaits(d):
        left = jnp.logical_and(d >= here, has_left)
        right = jnp.logical_and(d <= here, has_right)
        return left, right, jnp.logical_or(left, right)

    def send(step, slot, d, now):
        pl.when(jnp.logical_and(d > here, now))(lambda: right_copy(step, slot).start())
        pl.when(jnp.logical_and(d < here, now))(lambda: left_copy(step, slot).start())

    def join(step):
        d = target_of(step)
        give_copy(step).wait_recv()
        acc[step] += got[step]
        send(step, d * pieces + lax.rem(step, pieces), d, jnp.logical_not(awaits(d)[2]))

    def forward(step):
        d, piece = target_of(step), lax.rem(step, pieces)
        slot = d * pieces + piece
        left, right, some = awaits(d)

        @pl.when(left)
        def _():
            right_copy(step, slot).wait_recv()
            acc[step] += from_left[slot]

        @pl.when(right)
        def _():
            left_copy(step, slot).wait_recv()
            acc[step] += from_right[slot]

        send(step, slot, d, some)

        @pl.when(d == here)
        def _():
            out_ref[pl.ds(pl.multiple_of(piece * rows_piece, rows_piece), rows_piece), :] = acc[step]

    pl.loop(0, 2)(lay_out)
    q_copy(0).wait()

    @pl.loop(0, steps)
    def _(step):
        give[step] = part_of(step, 1 - core, 0, first_depth)
        acc[step] = part_of(step, core, 0, first_depth)

    pl.loop(2, cols + 1)(lay_out)
    q_copy(1).wait()
    rest = q_hbm.shape[0] - first_depth

    @pl.loop(0, steps)
    def _(step):
        give[step] += part_of(step, 1 - core, first_depth, rest)
        acc[step] += part_of(step, core, first_depth, rest)
        give_copy(step).start()
        pl.when(step > 0)(lambda: join(step - 1))
        pl.when(step > 1)(lambda: forward(step - 2))

    join(steps - 1)
    forward(steps - 2)
    forward(steps - 1)

    @pl.loop(0, steps)
    def _(step):
        d, piece = target_of(step), lax.rem(step, pieces)
        slot = d * pieces + piece
        give_copy(step).wait_send()
        pl.when(d > here)(lambda: right_copy(step, slot).wait_send())
        pl.when(d < here)(lambda: left_copy(step, slot).wait_send())

    @pl.loop(0, col + 1)
    def _(e):
        next_copy(e).wait_send()


def per_device(markov, panel):
    rows_here = markov.shape[0]
    n = lax.axis_size("rows")
    width_cols = rows_here // lax.axis_size("cols")
    sensors = panel.shape[0] // rows_here
    inputs = markov.shape[1] // sensors
    k = panel.shape[1]
    cols = lax.axis_size("cols")
    blocks_owned = width_cols // n
    pieces = 2 if blocks_owned % 4 == 0 else 1
    steps = (n // 2) * pieces
    tile = (steps, blocks_owned * inputs // pieces, k)
    dma = pltpu.SemaphoreType.DMA
    mine = pl.pallas_call(
        functools.partial(kernel, n, cols, inputs, blocks_owned, pieces),
        out_shape=jax.ShapeDtypeStruct((blocks_owned * inputs, k), jnp.float32),
        in_specs=[pl.BlockSpec(memory_space=pl.ANY)] * 2,
        out_specs=pl.BlockSpec(memory_space=pltpu.VMEM),
        scratch_shapes=[
            pltpu.VMEM((rows_here + width_cols, sensors * inputs), jnp.bfloat16),
            pltpu.VMEM((32 * sensors // 2, 128), jnp.float32),
            pltpu.VMEM((8 * sensors, 8 * sensors), jnp.bfloat16),
            pltpu.VMEM((2 * inputs, 128 + (rows_here + width_cols) * sensors), jnp.bfloat16),
            pltpu.VMEM(panel.shape, jnp.bfloat16),
        ]
        + [pltpu.VMEM(tile, jnp.float32)] * 5
        + [dma((cols,))] * 3
        + [dma((2,))]
        + [dma((steps,))] * 5,
        compiler_params=pltpu.CompilerParams(
            collective_id=0, has_side_effects=True, vmem_limit_bytes=56 * 2**20
        ),
        cost_estimate=pl.CostEstimate(
            flops=2 * width_cols * inputs * panel.shape[0] * k, bytes_accessed=16 * 2**20, transcendentals=0
        ),
    )(markov, panel)
    return mine[None]


def solution(mesh):
    placed = (P("rows", None), P("rows", None))
    return jax.shard_map(
        per_device, mesh=mesh, in_specs=placed, out_specs=P("cols", "rows", None), check_vma=False
    )
```

```python
import functools

import jax
import jax.numpy as jnp
from jax import lax
from jax.experimental import pallas as pl
from jax.experimental.pallas import tpu as pltpu
from jax.sharding import PartitionSpec as P

MESH = pl.DeviceIdType.MESH


def kernel(
    n, cols, inputs, blocks_owned, pieces,
    markov_hbm, q_hbm, out_ref,
    raw, spread, expand, ll_ref,
    q_ref, give, got, acc, from_left, from_right,
    near_sem, away_sem, next_sem, q_sem, give_sem, got_sem, line_sem, left_sem, right_sem,
):
    line = n // 2
    steps = line * pieces
    per_piece = blocks_owned // pieces
    rows_piece = per_piece * inputs
    width = markov_hbm.shape[0] // cols
    sensors = q_hbm.shape[0] // markov_hbm.shape[0]
    first_depth = width * sensors
    row, col = lax.axis_index("rows"), lax.axis_index("cols")
    here, core = row // 2, lax.rem(row, 2)
    sibling = row + 1 - 2 * core
    before, behind = lax.rem(row + n - 1, n), lax.rem(row + 1, n)
    has_left, has_right = here > 0, here < line - 1

    def q_copy(part):
        where = pl.ds(0, first_depth) if part == 0 else pl.ds(first_depth, q_hbm.shape[0] - first_depth)
        return pltpu.make_async_copy(q_hbm.at[where], q_ref.at[where], q_sem.at[part])

    def near_copy(g):
        src = pl.ds(pl.multiple_of((col + g) * width, width), width)
        dst = pl.ds(pl.multiple_of(g * width, width), width)
        return pltpu.make_async_copy(markov_hbm.at[src], raw.at[dst], near_sem.at[g])

    def next_copy(e):
        src = pl.ds(pl.multiple_of(e * width, width), width)
        dst = pl.ds(pl.multiple_of((e + cols - col) * width, width), width)
        return pltpu.make_async_remote_copy(
            markov_hbm.at[src], raw.at[dst], away_sem.at[e], next_sem.at[e],
            device_id={"rows": before}, device_id_type=MESH,
        )

    @pl.loop(0, cols - col)
    def _(g):
        near_copy(g).start()

    q_copy(0).start()
    q_copy(1).start()
    barrier = pltpu.get_barrier_semaphore()

    def greet(target):
        pl.semaphore_signal(barrier, inc=1, device_id={"rows": target}, device_id_type=MESH)

    greet(before)
    greet(behind)
    pl.when(has_left)(lambda: greet(row - 2))
    pl.when(has_right)(lambda: greet(row + 2))
    pl.semaphore_wait(barrier, 2 + jnp.where(has_left, 1, 0) + jnp.where(has_right, 1, 0))

    @pl.loop(0, col + 1)
    def _(e):
        next_copy(e).start()

    lane = 128
    half = expand.shape[0] // 2
    x = lax.broadcasted_iota(jnp.int32, expand.shape, 0)
    y = lax.broadcasted_iota(jnp.int32, expand.shape, 1)
    expand[...] = jnp.where(y == jnp.where(x < half, 2 * x, 2 * (x - half) + 1), 1.0, 0.0).astype(jnp.bfloat16)
    ll_ref[:, 0:lane] = jnp.zeros((2 * inputs, lane), jnp.bfloat16)
    group = 32
    pairs = sensors // 2

    def lay_out(g):
        pl.when(col + g < cols)(lambda: near_copy(g).wait())
        pl.when(col + g >= cols)(lambda: next_copy(col + g - cols).wait_recv())

        @pl.loop(0, width // group)
        def _(i):
            at = pl.multiple_of(g * width + i * group, group)
            for c in range(pairs):
                spread[pl.ds(c, group, stride=pairs), :] = raw[
                    pl.ds(at, group), c * lane : (c + 1) * lane
                ].astype(jnp.float32)
            turned = spread[...].astype(jnp.bfloat16).T
            lhs = jnp.concatenate(
                [
                    jnp.concatenate([turned[:inputs, k * half : (k + 1) * half], turned[inputs:, k * half : (k + 1) * half]], 1)
                    for k in range(2 * group // 16)
                ],
                0,
            )
            done = jnp.dot(lhs, expand[...], preferred_element_type=jnp.float32).astype(jnp.bfloat16)
            for k in range(2 * group // 16):
                to = pl.multiple_of(lane + at * sensors + k * 2 * half, lane)
                ll_ref[0:inputs, pl.ds(to, 2 * half)] = done[k * inputs : (k + 1) * inputs]

        span = 512

        @pl.loop(0, width * sensors // span)
        def _(i):
            at = pl.multiple_of(g * width * sensors + i * span, lane)
            wide = ll_ref[0:inputs, pl.ds(at, span + lane)]
            ll_ref[inputs : 2 * inputs, pl.ds(at, span)] = wide[:, sensors : sensors + span]

    def target_of(step):
        k = step // pieces
        low = here < line // 2
        h = jnp.where(low, here, line - 1 - here)
        d = jnp.where(k < line - 1 - h, line - 1 - k, jnp.where(k < line - 1, k - (line - 1 - h), h))
        return jnp.where(low, d, line - 1 - d)

    def part_of(step, core_of, begin, depth):
        d, piece = target_of(step), lax.rem(step, pieces)
        start = ((2 * d + core_of) * blocks_owned + piece * per_piece) * inputs + lane + begin
        parts = [
            ll_ref[:, pl.ds(pl.multiple_of(start + 2 * inputs * p, lane), depth)]
            for p in range(per_piece // 2)
        ]
        lhs = jnp.concatenate(parts, 0) if len(parts) > 1 else parts[0]
        return jnp.dot(lhs, q_ref[begin : begin + depth, :], preferred_element_type=jnp.float32)

    def give_copy(step):
        return pltpu.make_async_remote_copy(
            give.at[step], got.at[step], give_sem.at[step], got_sem.at[step],
            device_id={"rows": sibling}, device_id_type=MESH,
        )

    def right_copy(step, slot):
        return pltpu.make_async_remote_copy(
            acc.at[step], from_left.at[slot], line_sem.at[step], left_sem.at[slot],
            device_id={"rows": row + 2}, device_id_type=MESH,
        )

    def left_copy(step, slot):
        return pltpu.make_async_remote_copy(
            acc.at[step], from_right.at[slot], line_sem.at[step], right_sem.at[slot],
            device_id={"rows": row - 2}, device_id_type=MESH,
        )

    def awaits(d):
        left = jnp.logical_and(d >= here, has_left)
        right = jnp.logical_and(d <= here, has_right)
        return left, right, jnp.logical_or(left, right)

    def send(step, slot, d, now):
        pl.when(jnp.logical_and(d > here, now))(lambda: right_copy(step, slot).start())
        pl.when(jnp.logical_and(d < here, now))(lambda: left_copy(step, slot).start())

    def join(step):
        d = target_of(step)
        give_copy(step).wait_recv()
        acc[step] += got[step]
        send(step, d * pieces + lax.rem(step, pieces), d, jnp.logical_not(awaits(d)[2]))

    def forward(step):
        d, piece = target_of(step), lax.rem(step, pieces)
        slot = d * pieces + piece
        left, right, some = awaits(d)

        @pl.when(left)
        def _():
            right_copy(step, slot).wait_recv()
            acc[step] += from_left[slot]

        @pl.when(right)
        def _():
            left_copy(step, slot).wait_recv()
            acc[step] += from_right[slot]

        send(step, slot, d, some)

        @pl.when(d == here)
        def _():
            out_ref[pl.ds(pl.multiple_of(piece * rows_piece, rows_piece), rows_piece), :] = acc[step]

    pl.loop(0, cols + 1)(lay_out)
    q_copy(0).wait()
    q_copy(1).wait()
    whole = q_hbm.shape[0]

    @pl.loop(0, steps)
    def _(step):
        give[step] = part_of(step, 1 - core, 0, whole)
        acc[step] = part_of(step, core, 0, whole)
        give_copy(step).start()
        pl.when(step > 0)(lambda: join(step - 1))
        pl.when(step > 1)(lambda: forward(step - 2))

    join(steps - 1)
    forward(steps - 2)
    forward(steps - 1)

    @pl.loop(0, steps)
    def _(step):
        d, piece = target_of(step), lax.rem(step, pieces)
        slot = d * pieces + piece
        give_copy(step).wait_send()
        pl.when(d > here)(lambda: right_copy(step, slot).wait_send())
        pl.when(d < here)(lambda: left_copy(step, slot).wait_send())

    @pl.loop(0, col + 1)
    def _(e):
        next_copy(e).wait_send()


def per_device(markov, panel):
    rows_here = markov.shape[0]
    n = lax.axis_size("rows")
    width_cols = rows_here // lax.axis_size("cols")
    sensors = panel.shape[0] // rows_here
    inputs = markov.shape[1] // sensors
    k = panel.shape[1]
    cols = lax.axis_size("cols")
    blocks_owned = width_cols // n
    pieces = 2 if blocks_owned % 4 == 0 else 1
    steps = (n // 2) * pieces
    tile = (steps, blocks_owned * inputs // pieces, k)
    dma = pltpu.SemaphoreType.DMA
    mine = pl.pallas_call(
        functools.partial(kernel, n, cols, inputs, blocks_owned, pieces),
        out_shape=jax.ShapeDtypeStruct((blocks_owned * inputs, k), jnp.float32),
        in_specs=[pl.BlockSpec(memory_space=pl.ANY)] * 2,
        out_specs=pl.BlockSpec(memory_space=pltpu.VMEM),
        scratch_shapes=[
            pltpu.VMEM((rows_here + width_cols, sensors * inputs), jnp.bfloat16),
            pltpu.VMEM((32 * sensors // 2, 128), jnp.float32),
            pltpu.VMEM((8 * sensors, 8 * sensors), jnp.bfloat16),
            pltpu.VMEM((2 * inputs, 128 + (rows_here + width_cols) * sensors), jnp.bfloat16),
            pltpu.VMEM(panel.shape, jnp.bfloat16),
        ]
        + [pltpu.VMEM(tile, jnp.float32)] * 5
        + [dma((cols,))] * 3
        + [dma((2,))]
        + [dma((steps,))] * 5,
        compiler_params=pltpu.CompilerParams(
            collective_id=0, has_side_effects=True, vmem_limit_bytes=56 * 2**20
        ),
        cost_estimate=pl.CostEstimate(
            flops=2 * width_cols * inputs * panel.shape[0] * k, bytes_accessed=16 * 2**20, transcendentals=0
        ),
    )(markov, panel)
    return mine[None]


def solution(mesh):
    placed = (P("rows", None), P("rows", None))
    return jax.shard_map(
        per_device, mesh=mesh, in_specs=placed, out_specs=P("cols", "rows", None), check_vma=False
    )
```
